32 devices in a mesh: fsdp: 8 (over z, y), tp: 4 (over x, core).
Axes of the slice: x: 2, y: 2, z: 4, core: 2. Of those that a mesh axis runs over, the one named last changes fastest.
Arguments:
- gradient: bfloat16 [768, 1280], P('fsdp', 'tp'), may hold values from -6 to 6
- momentum: float32 [768, 1280], P('fsdp', 'tp'), may hold values from -6 to 6
- q_factor: float32 [4, 320, 128], P('tp', 'fsdp'), may hold values from -6 to 6
Outputs:
- momentum_out: float32 [768, 1280], P('fsdp', 'tp')
- q_out: float32 [4, 320, 128], P('tp', 'fsdp')
- update: bfloat16 [768, 1280], P('fsdp', 'tp')
The draws below stay inside these ranges and needn't reach their ends.
All inputs are finite; a program needn't handle non-finite values.
Results may differ from the reference program's by a relative error of at most 0.001.
Values sent between devices are 32-bit elements; how exact they have to be, the bound alone decides.
A program may use at most 64 MiB of HBM per device.

```python
import jax
import jax.numpy as jnp
from jax import lax

RANK = 128
ROWS = 768
COLS = 1280
CT = 320
N_TP = 4


def block_levels(key, dims, pieces, low, top_value):
    loudness, own = 1.0, jax.random.fold_in(key, 6)
    for position, parts in pieces:
        heights = jnp.exp(jax.random.uniform(jax.random.fold_in(own, position), (parts,), jnp.float32, low / len(pieces), top_value / len(pieces)))
        loudness = loudness * jnp.repeat(heights, dims[position] // parts).reshape([-1 if axis == position else 1 for axis in range(len(dims))])
    return loudness


def normal_values(own_key, extent, spread, reach, cuts=(), held_as=jnp.bfloat16):
    loudness = block_levels(own_key, extent, cuts, -0.22, 0.18) if cuts else 1.0
    result = jax.random.normal(own_key, extent, jnp.float32) * spread * loudness
    return jnp.minimum(jnp.maximum(result, -reach), reach).astype(held_as)


def setup_inputs(seed: int = 0) -> dict:
    key_list = jax.random.split(jax.random.key(seed), 4)
    gradient = normal_values(key_list[0], (ROWS, COLS), 1.0, 6.0, ((0, 8), (1, 4)))
    momentum = normal_values(key_list[1], (ROWS, COLS), 1.0, 6.0, ((0, 8), (1, 4)), jnp.float32)
    q_factor = normal_values(key_list[2], (N_TP, CT, RANK), 1.0, 6.0, ((0, 4), (1, 8)), jnp.float32)
    return dict(gradient=gradient, momentum=momentum, q_factor=q_factor)


def reference(gradient, momentum, q_factor):
    high = lax.Precision.HIGHEST
    q = q_factor.reshape(COLS, RANK)
    buffer = momentum + gradient.astype(jnp.float32)
    left = jnp.dot(buffer.astype(jnp.float32), q.astype(jnp.float32), precision=high, preferred_element_type=jnp.float32)
    gram = jnp.dot(left.T.astype(jnp.float32), left.astype(jnp.float32), precision=high, preferred_element_type=jnp.float32)
    lower = jnp.linalg.cholesky(gram)
    basis = jax.scipy.linalg.solve_triangular(lower, left.T, lower=True).T
    right = jnp.dot(buffer.T.astype(jnp.float32), basis.astype(jnp.float32), precision=high, preferred_element_type=jnp.float32)
    colscale = jnp.sqrt(lax.optimization_barrier(jnp.sum(right * right, axis=0)) / COLS + 1e-06)
    q_new = right / colscale
    feedback = buffer - 0.05 * jnp.dot((basis * colscale).astype(jnp.float32), q_new.T.astype(jnp.float32), precision=high, preferred_element_type=jnp.float32)
    update = (jnp.sqrt(ROWS / RANK) * jnp.dot(basis.astype(jnp.float32), q_new.T.astype(jnp.float32), precision=high, preferred_element_type=jnp.float32)).astype(jnp.bfloat16)
    return (feedback, q_new.reshape(N_TP, CT, RANK), update)
```

```python
import functools

import jax
import jax.numpy as jnp
from jax import lax
from jax.experimental import pallas as pl
from jax.experimental.pallas import tpu as pltpu
from jax.sharding import PartitionSpec as P

MESH = pl.DeviceIdType.MESH
HIGH = lax.Precision.HIGHEST
F32 = jnp.float32
BLOCK = 16


def dot(a, b, ca, cb):
    return lax.dot_general(
        a, b, (((ca,), (cb,)), ((), ())), precision=HIGH, preferred_element_type=F32
    )


def each(start, stop, body):
    if stop - start <= 8:
        for i in range(start, stop):
            body(i)
    else:
        def step(i, carry):
            body(i)
            return carry
        lax.fori_loop(start, stop, step, 0)


def sum_slots(ref, count):
    if count <= 8:
        total = ref[0]
        for i in range(1, count):
            total = total + ref[i]
        return total
    return lax.fori_loop(1, count, lambda i, s: s + ref[i], ref[0])


def factor_block(rows_a, rows_e, first):
    b, rank = rows_a.shape
    index = lax.broadcasted_iota(jnp.int32, (b, rank), 0)
    wide = jnp.stack(
        [jnp.broadcast_to(rows_a[:, first + j : first + j + 1], (b, rank)) for j in range(b)]
    )
    scale = jnp.zeros((b, rank), F32)
    for k in range(b):
        column = wide[0]
        root = lax.rsqrt(column[k : k + 1, :])
        scale = jnp.where(index == k, root, scale)
        if k < b - 1:
            factor = jnp.where(index > k, column * (root * root), 0.0)
            rows_a = rows_a - factor * rows_a[k : k + 1, :]
            rows_e = rows_e - factor * rows_e[k : k + 1, :]
            wide = wide[1:] - factor[None] * wide[1:, k : k + 1, :]
    return rows_a * scale, rows_e * scale


def factor_range(a, e, done, first, last):
    rank = a.shape[1]
    for block in range(first, last):
        at = block * BLOCK
        upper, inverse = factor_block(a[:BLOCK], e[:BLOCK], at)
        done.append(inverse)
        if at + BLOCK < rank:
            lower = upper.T[at + BLOCK :]
            change = dot(lower, jnp.concatenate([upper, inverse], axis=1), 1, 0)
            a = a[BLOCK:] - change[:, :rank]
            e = e[BLOCK:] - change[:, rank:]
    return a, e


def kernel(
    nf, nt, rows_total, cols_total, chunk,
    grad_ref, mom_ref, q_ref, mom_out, q_out, upd_out,
    buf, q_all, parts, gram, gram_in, gram_all, m_part, m_in, m_all, right_all, sq_in,
    qs, qr, ps, pr, gs, gr, hs, hr, ms, mr, fs, fr, ss, sr,
):
    f, t = lax.axis_index("fsdp"), lax.axis_index("tp")
    rows, cols = mom_ref.shape
    kr, rank = q_ref.shape[1], q_ref.shape[2]
    gq = rank // nt
    n_chunks = cols // chunk

    def fpeer(d):
        return (lax.rem(f + d, nf), t)

    def tpeer(d):
        return (f, lax.rem(t + d, nt))

    def copy(src, dst, send, recv, d, peer):
        return pltpu.make_async_remote_copy(
            src_ref=src, dst_ref=dst, send_sem=send.at[d], recv_sem=recv.at[d],
            device_id=peer, device_id_type=MESH,
        )

    def q_copy(d):
        return copy(q_ref.at[0], q_all.at[f], qs, qr, d, fpeer(d))

    def p_copy(d):
        return copy(parts.at[t], parts.at[t], ps, pr, d, tpeer(d))

    mine = pl.ds(pl.multiple_of(t * gq, 8), gq)

    def g_copy(d):
        return copy(gram.at[mine], gram_in.at[f], gs, gr, d, fpeer(d))

    def h_copy(d):
        return copy(gram_all.at[t], gram_all.at[t], hs, hr, d, tpeer(d))

    def m_copy(d):
        return copy(m_part.at[lax.rem(f + d, nf)], m_in.at[f], ms, mr, d, fpeer(d))

    def f_copy(d):
        return copy(m_all.at[f], m_all.at[f], fs, fr, d, fpeer(d))

    def s_copy(d):
        return copy(sq_in.at[t], sq_in.at[t], ss, sr, d, tpeer(d))

    def columns(body):
        if n_chunks == 1:
            body(slice(None), slice(None))
        else:
            def step(i, carry):
                at = pl.ds(pl.multiple_of(i * chunk, 128), chunk)
                body(at, at)
                return carry
            lax.fori_loop(0, n_chunks, step, 0)

    barrier = pltpu.get_barrier_semaphore()
    each(1, nf, lambda d: pl.semaphore_signal(barrier, inc=1, device_id=fpeer(d), device_id_type=MESH))
    each(1, nt, lambda d: pl.semaphore_signal(barrier, inc=1, device_id=tpeer(d), device_id_type=MESH))
    pl.semaphore_wait(barrier, nf - 1 + nt - 1)

    each(1, nf, lambda d: q_copy(d).start())
    q_all[f] = q_ref[0]
    buf[...] = mom_ref[...] + grad_ref[...].astype(F32)
    each(1, nf, lambda d: q_copy(d).wait_recv())

    if n_chunks == 1:
        parts[t] = dot(buf[...], q_all[...].reshape(cols, rank), 1, 0)
    else:
        per = chunk // kr
        def left_step(i, total):
            at = pl.ds(pl.multiple_of(i * chunk, 128), chunk)
            return total + dot(buf[:, at], q_all[pl.ds(i * per, per)].reshape(chunk, rank), 1, 0)
        parts[t] = lax.fori_loop(0, n_chunks, left_step, jnp.zeros((rows, rank), F32))
    each(1, nt, lambda d: p_copy(d).start())
    each(1, nt, lambda d: p_copy(d).wait_recv())
    left = sum_slots(parts, nt)

    gram[...] = dot(left, left, 0, 0)
    each(1, nf, lambda d: g_copy(d).start())
    gram_in[f] = gram[mine]

    if n_chunks == 1:
        m_part[...] = dot(buf[...], left, 0, 0).reshape(nf, kr, rank)
    else:
        per = chunk // kr
        def m_step(i, carry):
            at = pl.ds(pl.multiple_of(i * chunk, 128), chunk)
            m_part[pl.ds(i * per, per)] = dot(buf[:, at], left, 0, 0).reshape(per, kr, rank)
            return carry
        lax.fori_loop(0, n_chunks, m_step, 0)
    each(1, nf, lambda d: m_copy(d).start())
    m_in[f] = m_part[f]

    each(1, nf, lambda d: g_copy(d).wait_recv())
    gram_all[t] = sum_slots(gram_in, nf)
    each(1, nt, lambda d: h_copy(d).start())
    each(1, nt, lambda d: h_copy(d).wait_recv())

    a = gram_all[...].reshape(rank, rank)
    row_id = lax.broadcasted_iota(jnp.int32, (rank, rank), 0)
    col_id = lax.broadcasted_iota(jnp.int32, (rank, rank), 1)
    e = jnp.where(row_id == col_id, 1.0, 0.0).astype(F32)
    blocks = rank // BLOCK
    done = []
    a, e = factor_range(a, e, done, 0, blocks // 2)
    each(1, nf, lambda d: m_copy(d).wait_recv())
    m_all[f] = sum_slots(m_in, nf)
    each(1, nf, lambda d: f_copy(d).start())
    factor_range(a, e, done, blocks // 2, blocks)
    inverse = jnp.concatenate(done, axis=0)
    each(1, nf, lambda d: f_copy(d).wait_recv())

    basis = dot(left, inverse, 1, 1)
    if n_chunks == 1:
        right = dot(m_all[...].reshape(cols, rank), inverse, 1, 1)
        right_all[...] = right
        squares = jnp.sum(right * right, axis=0, keepdims=True)
    else:
        per = chunk // kr
        def right_step(i, total):
            at = pl.ds(pl.multiple_of(i * chunk, 128), chunk)
            right = dot(m_all[pl.ds(i * per, per)].reshape(chunk, rank), inverse, 1, 1)
            right_all[at] = right
            return total + jnp.sum(right * right, axis=0, keepdims=True)
        squares = lax.fori_loop(0, n_chunks, right_step, jnp.zeros((1, rank), F32))
    sq_in[t] = jnp.broadcast_to(squares, (8, rank))
    each(1, nt, lambda d: s_copy(d).start())

    def feedback(at, rat):
        mom_out[:, at] = buf[:, at] - 0.05 * dot(basis, right_all[rat], 1, 1)
    columns(feedback)

    each(1, nt, lambda d: s_copy(d).wait_recv())
    colscale = jnp.sqrt(sum_slots(sq_in, nt)[0:1] / cols_total + 1e-06)
    own = right_all[pl.ds(pl.multiple_of(f * kr, 8), kr)]
    q_out[0] = own / colscale
    scaled = basis * ((rows_total / rank) ** 0.5) / colscale

    def direction(at, rat):
        upd_out[:, at] = dot(scaled, right_all[rat], 1, 1).astype(jnp.bfloat16)
    columns(direction)

    for c in (q_copy, g_copy, m_copy, f_copy):
        each(1, nf, lambda d: c(d).wait_send())
    for c in (p_copy, h_copy, s_copy):
        each(1, nt, lambda d: c(d).wait_send())


def per_device(nf, nt, gradient, momentum, q_factor):
    rows, cols = momentum.shape
    kr, rank = q_factor.shape[1], q_factor.shape[2]
    chunk = 640 if cols > 640 and cols % 640 == 0 and 640 % kr == 0 else cols
    sem = pltpu.SemaphoreType.DMA
    vmem = pl.BlockSpec(memory_space=pltpu.VMEM)
    return pl.pallas_call(
        functools.partial(kernel, nf, nt, rows * nf, cols * nt, chunk),
        out_shape=(
            jax.ShapeDtypeStruct((rows, cols), F32),
            jax.ShapeDtypeStruct((1, kr, rank), F32),
            jax.ShapeDtypeStruct((rows, cols), jnp.bfloat16),
        ),
        in_specs=[vmem] * 3,
        out_specs=(vmem,) * 3,
        scratch_shapes=[
            pltpu.VMEM((rows, cols), F32),
            pltpu.VMEM((nf, kr, rank), F32),
            pltpu.VMEM((nt, rows, rank), F32),
            pltpu.VMEM((rank, rank), F32),
            pltpu.VMEM((nf, rank // nt, rank), F32),
            pltpu.VMEM((nt, rank // nt, rank), F32),
            pltpu.VMEM((nf, kr, rank), F32),
            pltpu.VMEM((nf, kr, rank), F32),
            pltpu.VMEM((nf, kr, rank), F32),
            pltpu.VMEM((cols, rank), F32),
            pltpu.VMEM((nt, 8, rank), F32),
        ]
        + [sem((nf,)), sem((nf,)), sem((nt,)), sem((nt,)), sem((nf,)), sem((nf,)), sem((nt,)), sem((nt,))]
        + [sem((nf,)), sem((nf,)), sem((nf,)), sem((nf,)), sem((nt,)), sem((nt,))],
        compiler_params=pltpu.CompilerParams(
            collective_id=0, has_side_effects=True, vmem_limit_bytes=40 * 1024 * 1024
        ),
    )(gradient, momentum, q_factor)


def solution(mesh):
    placed = (P("fsdp", "tp"), P("fsdp", "tp"), P("tp", "fsdp", None))
    return jax.shard_map(
        functools.partial(per_device, mesh.shape["fsdp"], mesh.shape["tp"]),
        mesh=mesh,
        in_specs=placed,
        out_specs=(P("fsdp", "tp"), P("tp", "fsdp", None), P("fsdp", "tp")),
        check_vma=False,
    )
```

```python
import functools

import jax
import jax.numpy as jnp
from jax import lax
from jax.experimental import pallas as pl
from jax.experimental.pallas import tpu as pltpu
from jax.sharding import PartitionSpec as P

MESH = pl.DeviceIdType.MESH
HIGH = lax.Precision.HIGHEST
F32 = jnp.float32
BLOCK = 16


def dot(a, b, ca, cb):
    return lax.dot_general(
        a, b, (((ca,), (cb,)), ((), ())), precision=HIGH, preferred_element_type=F32
    )


def each(start, stop, body):
    if stop - start <= 8:
        for i in range(start, stop):
            body(i)
    else:
        def step(i, carry):
            body(i)
            return carry
        lax.fori_loop(start, stop, step, 0)


def sum_slots(ref, count):
    if count <= 8:
        total = ref[0]
        for i in range(1, count):
            total = total + ref[i]
        return total
    return lax.fori_loop(1, count, lambda i, s: s + ref[i], ref[0])


def factor_block(rows_a, rows_e, first):
    b, rank = rows_a.shape
    index = lax.broadcasted_iota(jnp.int32, (b, rank), 0)
    wide = jnp.stack(
        [jnp.broadcast_to(rows_a[:, first + j : first + j + 1], (b, rank)) for j in range(b)]
    )
    scale = jnp.zeros((b, rank), F32)
    for k in range(b):
        column = wide[0]
        root = lax.rsqrt(column[k : k + 1, :])
        scale = jnp.where(index == k, root, scale)
        if k < b - 1:
            factor = jnp.where(index > k, column * (root * root), 0.0)
            rows_a = rows_a - factor * rows_a[k : k + 1, :]
            rows_e = rows_e - factor * rows_e[k : k + 1, :]
            wide = wide[1:] - factor[None] * wide[1:, k : k + 1, :]
    return rows_a * scale, rows_e * scale


def split(x):
    high = x.astype(jnp.bfloat16)
    rest = x - high.astype(F32)
    mid = rest.astype(jnp.bfloat16)
    return high, mid, (rest - mid.astype(F32)).astype(jnp.bfloat16)


def factor_range(a, e, done, first, last):
    rank = a.shape[1]
    for block in range(first, last):
        at = block * BLOCK
        upper, inverse = factor_block(a[:BLOCK], e[:BLOCK], at)
        done.append(inverse)
        if at + BLOCK < rank:
            h, m, l = split(jnp.concatenate([upper, inverse], axis=1))
            hu, mu, lu = h[:, :rank], m[:, :rank], l[:, :rank]
            lhs = jnp.concatenate([hu, hu, mu, mu, hu, lu], axis=0)
            rhs = jnp.concatenate([h, m, h, m, l, h], axis=0)
            change = lax.dot_general(
                lhs, rhs, (((0,), (0,)), ((), ())), preferred_element_type=F32
            )[at + BLOCK :]
            a = a[BLOCK:] - change[:, :rank]
            e = e[BLOCK:] - change[:, rank:]
    return a, e


def kernel(
    nf, nt, rows_total, cols_total, chunk,
    grad_hbm, mom_hbm, q_ref, mom_out, q_out, scaled_out, right_all,
    grad_ref, mom_ref, buf, q_all, parts, gram, gram_in, gram_all, m_part, m_in, m_all, sq_in,
    qs, qr, ps, pr, gs, gr, hs, hr, ms, mr, fs, fr, ss, sr, local,
):
    f, t = lax.axis_index("fsdp"), lax.axis_index("tp")
    rows, cols = mom_ref.shape
    kr, rank = q_ref.shape[1], q_ref.shape[2]
    gq = rank // nt
    n_chunks = cols // chunk

    def fpeer(d):
        return (lax.rem(f + d, nf), t)

    def tpeer(d):
        return (f, lax.rem(t + d, nt))

    def copy(src, dst, send, recv, d, peer):
        return pltpu.make_async_remote_copy(
            src_ref=src, dst_ref=dst, send_sem=send.at[d], recv_sem=recv.at[d],
            device_id=peer, device_id_type=MESH,
        )

    def q_copy(d):
        return copy(q_ref.at[0], q_all.at[f], qs, qr, d, fpeer(d))

    def p_copy(d):
        return copy(parts.at[t], parts.at[t], ps, pr, d, tpeer(d))

    mine = pl.ds(pl.multiple_of(t * gq, 8), gq)

    def g_copy(d):
        return copy(gram.at[mine], gram_in.at[f], gs, gr, d, fpeer(d))

    def h_copy(d):
        return copy(gram_all.at[t], gram_all.at[t], hs, hr, d, tpeer(d))

    def m_copy(d):
        return copy(m_part.at[lax.rem(f + d, nf)], m_in.at[f], ms, mr, d, fpeer(d))

    def f_copy(d):
        return copy(m_all.at[f], m_all.at[f], fs, fr, d, fpeer(d))

    def s_copy(d):
        return copy(sq_in.at[t], sq_in.at[t], ss, sr, d, tpeer(d))

    def columns(body):
        if n_chunks == 1:
            body(slice(None), slice(None))
        else:
            def step(i, carry):
                at = pl.ds(pl.multiple_of(i * chunk, 128), chunk)
                body(at, at)
                return carry
            lax.fori_loop(0, n_chunks, step, 0)

    grad_copy = pltpu.make_async_copy(grad_hbm, grad_ref, local.at[0])
    mom_copy = pltpu.make_async_copy(mom_hbm, mom_ref, local.at[1])
    own_copy = pltpu.make_async_copy(q_ref.at[0], q_all.at[f], local.at[2])
    own_copy.start()
    mom_copy.start()
    grad_copy.start()

    barrier = pltpu.get_barrier_semaphore()
    each(1, nf, lambda d: pl.semaphore_signal(barrier, inc=1, device_id=fpeer(d), device_id_type=MESH))
    each(1, nt, lambda d: pl.semaphore_signal(barrier, inc=1, device_id=tpeer(d), device_id_type=MESH))
    pl.semaphore_wait(barrier, nf - 1 + nt - 1)

    each(1, nf, lambda d: q_copy(d).start())
    mom_copy.wait()
    grad_copy.wait()
    buf[...] = mom_ref[...] + grad_ref[...].astype(F32)
    own_copy.wait()
    each(1, nf, lambda d: q_copy(d).wait_recv())

    if n_chunks == 1:
        parts[t] = dot(buf[...], q_all[...].reshape(cols, rank), 1, 0)
    else:
        per = chunk // kr
        def left_step(i, total):
            at = pl.ds(pl.multiple_of(i * chunk, 128), chunk)
            return total + dot(buf[:, at], q_all[pl.ds(i * per, per)].reshape(chunk, rank), 1, 0)
        parts[t] = lax.fori_loop(0, n_chunks, left_step, jnp.zeros((rows, rank), F32))
    each(1, nt, lambda d: p_copy(d).start())
    each(1, nt, lambda d: p_copy(d).wait_recv())
    left = sum_slots(parts, nt)

    gram[...] = dot(left, left, 0, 0)
    each(1, nf, lambda d: g_copy(d).start())
    gram_in[f] = gram[mine]

    if n_chunks == 1:
        m_part[...] = dot(buf[...], left, 0, 0).reshape(nf, kr, rank)
    else:
        per = chunk // kr
        def m_step(i, carry):
            at = pl.ds(pl.multiple_of(i * chunk, 128), chunk)
            m_part[pl.ds(i * per, per)] = dot(buf[:, at], left, 0, 0).reshape(per, kr, rank)
            return carry
        lax.fori_loop(0, n_chunks, m_step, 0)
    each(1, nf, lambda d: m_copy(d).start())
    m_in[f] = m_part[f]

    each(1, nf, lambda d: g_copy(d).wait_recv())
    gram_all[t] = sum_slots(gram_in, nf)
    each(1, nt, lambda d: h_copy(d).start())
    each(1, nf, lambda d: m_copy(d).wait_recv())
    m_all[f] = sum_slots(m_in, nf)
    each(1, nf, lambda d: f_copy(d).start())
    each(1, nt, lambda d: h_copy(d).wait_recv())

    a = gram_all[...].reshape(rank, rank)
    row_id = lax.broadcasted_iota(jnp.int32, (rank, rank), 0)
    col_id = lax.broadcasted_iota(jnp.int32, (rank, rank), 1)
    e = jnp.where(row_id == col_id, 1.0, 0.0).astype(F32)
    blocks = rank // BLOCK
    done = []
    a, e = factor_range(a, e, done, 0, blocks // 2)
    factor_range(a, e, done, blocks // 2, blocks)
    inverse = jnp.concatenate(done, axis=0)
    each(1, nf, lambda d: f_copy(d).wait_recv())

    basis = dot(left, inverse, 1, 1)
    if n_chunks == 1:
        right = dot(m_all[...].reshape(cols, rank), inverse, 1, 1)
        right_all[...] = right
        squares = jnp.sum(right * right, axis=0, keepdims=True)
    else:
        per = chunk // kr
        def right_step(i, total):
            at = pl.ds(pl.multiple_of(i * chunk, 128), chunk)
            right = dot(m_all[pl.ds(i * per, per)].reshape(chunk, rank), inverse, 1, 1)
            right_all[at] = right
            return total + jnp.sum(right * right, axis=0, keepdims=True)
        squares = lax.fori_loop(0, n_chunks, right_step, jnp.zeros((1, rank), F32))
    sq_in[t] = jnp.broadcast_to(squares, (8, rank))
    each(1, nt, lambda d: s_copy(d).start())

    def feedback(at, rat):
        mom_out[:, at] = buf[:, at] - 0.05 * dot(basis, right_all[rat], 1, 1)
    columns(feedback)

    each(1, nt, lambda d: s_copy(d).wait_recv())
    colscale = jnp.sqrt(sum_slots(sq_in, nt)[0:1] / cols_total + 1e-06)
    own = right_all[pl.ds(pl.multiple_of(f * kr, 8), kr)]
    q_out[0] = own / colscale
    scaled_out[...] = basis * ((rows_total / rank) ** 0.5) / colscale

    for c in (q_copy, g_copy, m_copy, f_copy):
        each(1, nf, lambda d: c(d).wait_send())
    for c in (p_copy, h_copy, s_copy):
        each(1, nt, lambda d: c(d).wait_send())


def finish(chunk, mom_ref, q_ref, scaled_ref, right_ref, mom_out, q_out, upd_out, upd, sem):
    mom_copy = pltpu.make_async_copy(mom_ref, mom_out, sem.at[0])
    q_copy = pltpu.make_async_copy(q_ref, q_out, sem.at[1])
    mom_copy.start()
    q_copy.start()
    scaled = scaled_ref[...]
    cols = upd.shape[1]
    if cols == chunk:
        upd[...] = dot(scaled, right_ref[...], 1, 1).astype(jnp.bfloat16)
    else:
        def step(i, carry):
            at = pl.ds(pl.multiple_of(i * chunk, 128), chunk)
            upd[:, at] = dot(scaled, right_ref[at], 1, 1).astype(jnp.bfloat16)
            return carry
        lax.fori_loop(0, cols // chunk, step, 0)
    upd_copy = pltpu.make_async_copy(upd, upd_out, sem.at[2])
    upd_copy.start()
    mom_copy.wait()
    q_copy.wait()
    upd_copy.wait()


def per_device(nf, nt, gradient, momentum, q_factor):
    rows, cols = momentum.shape
    kr, rank = q_factor.shape[1], q_factor.shape[2]
    chunk = 640 if cols > 640 and cols % 640 == 0 and 640 % kr == 0 else cols
    sem = pltpu.SemaphoreType.DMA
    vmem = pl.BlockSpec(memory_space=pltpu.VMEM)
    hbm = pl.BlockSpec(memory_space=pl.ANY)
    mom, q_new, scaled, right = pl.pallas_call(
        functools.partial(kernel, nf, nt, rows * nf, cols * nt, chunk),
        out_shape=(
            jax.ShapeDtypeStruct((rows, cols), F32),
            jax.ShapeDtypeStruct((1, kr, rank), F32),
            jax.ShapeDtypeStruct((rows, rank), F32),
            jax.ShapeDtypeStruct((cols, rank), F32),
        ),
        in_specs=[pl.BlockSpec(memory_space=pltpu.HBM)] * 3,
        out_specs=(vmem,) * 4,
        scratch_shapes=[
            pltpu.VMEM((rows, cols), jnp.bfloat16),
            pltpu.VMEM((rows, cols), F32),
            pltpu.VMEM((rows, cols), F32),
            pltpu.VMEM((nf, kr, rank), F32),
            pltpu.VMEM((nt, rows, rank), F32),
            pltpu.VMEM((rank, rank), F32),
            pltpu.VMEM((nf, rank // nt, rank), F32),
            pltpu.VMEM((nt, rank // nt, rank), F32),
            pltpu.VMEM((nf, kr, rank), F32),
            pltpu.VMEM((nf, kr, rank), F32),
            pltpu.VMEM((nf, kr, rank), F32),
            pltpu.VMEM((nt, 8, rank), F32),
        ]
        + [sem((nf,)), sem((nf,)), sem((nt,)), sem((nt,)), sem((nf,)), sem((nf,)), sem((nt,)), sem((nt,))]
        + [sem((nf,)), sem((nf,)), sem((nf,)), sem((nf,)), sem((nt,)), sem((nt,)), sem((3,))],
        compiler_params=pltpu.CompilerParams(
            collective_id=0, has_side_effects=True, vmem_limit_bytes=40 * 1024 * 1024
        ),
    )(*[pltpu.with_memory_space_constraint(x, pltpu.HBM) for x in (gradient, momentum, q_factor)])
    return pl.pallas_call(
        functools.partial(finish, chunk),
        out_shape=(
            jax.ShapeDtypeStruct((rows, cols), F32),
            jax.ShapeDtypeStruct((1, kr, rank), F32),
            jax.ShapeDtypeStruct((rows, cols), jnp.bfloat16),
        ),
        in_specs=[vmem] * 4,
        out_specs=(hbm,) * 3,
        scratch_shapes=[pltpu.VMEM((rows, cols), jnp.bfloat16), sem((3,))],
        compiler_params=pltpu.CompilerParams(vmem_limit_bytes=16 * 1024 * 1024),
    )(mom, q_new, scaled, right)


def solution(mesh):
    placed = (P("fsdp", "tp"), P("fsdp", "tp"), P("tp", "fsdp", None))
    return jax.shard_map(
        functools.partial(per_device, mesh.shape["fsdp"], mesh.shape["tp"]),
        mesh=mesh,
        in_specs=placed,
        out_specs=(P("fsdp", "tp"), P("tp", "fsdp", None), P("fsdp", "tp")),
        check_vma=False,
    )
```

```python
import functools

import jax
import jax.numpy as jnp
from jax import lax
from jax.experimental import pallas as pl
from jax.experimental.pallas import tpu as pltpu
from jax.sharding import PartitionSpec as P

MESH = pl.DeviceIdType.MESH
HIGH = lax.Precision.HIGHEST
F32 = jnp.float32
BLOCK = 16


def dot(a, b, ca, cb):
    return lax.dot_general(
        a, b, (((ca,), (cb,)), ((), ())), precision=HIGH, preferred_element_type=F32
    )


def dot3(a, b):
    h, m, _ = split(a)
    u, v, _ = split(b)
    def one(x, y):
        return lax.dot_general(x, y, (((1,), (1,)), ((), ())), preferred_element_type=F32)
    return one(h, v) + one(m, u) + one(h, u)


def each(start, stop, body):
    if stop - start <= 8:
        for i in range(start, stop):
            body(i)
    else:
        def step(i, carry):
            body(i)
            return carry
        lax.fori_loop(start, stop, step, 0)


def sum_slots(ref, count):
    if count <= 8:
        total = ref[0]
        for i in range(1, count):
            total = total + ref[i]
        return total
    return lax.fori_loop(1, count, lambda i, s: s + ref[i], ref[0])


def factor_block(rows_a, rows_e, first):
    b, rank = rows_a.shape
    index = lax.broadcasted_iota(jnp.int32, (b, rank), 0)
    wide = jnp.stack(
        [jnp.broadcast_to(rows_a[:, first + j : first + j + 1], (b, rank)) for j in range(b)]
    )
    scale = jnp.zeros((b, rank), F32)
    for k in range(b):
        column = wide[0]
        root = lax.rsqrt(column[k : k + 1, :])
        scale = jnp.where(index == k, root, scale)
        if k < b - 1:
            factor = jnp.where(index > k, column * (root * root), 0.0)
            rows_a = rows_a - factor * rows_a[k : k + 1, :]
            rows_e = rows_e - factor * rows_e[k : k + 1, :]
            wide = wide[1:] - factor[None] * wide[1:, k : k + 1, :]
    return rows_a * scale, rows_e * scale


def split(x):
    high = x.astype(jnp.bfloat16)
    rest = x - high.astype(F32)
    mid = rest.astype(jnp.bfloat16)
    return high, mid, (rest - mid.astype(F32)).astype(jnp.bfloat16)


def factor_range(a, e, done, first, last):
    rank = a.shape[1]
    for block in range(first, last):
        at = block * BLOCK
        upper, inverse = factor_block(a[:BLOCK], e[:BLOCK], at)
        done.append(inverse)
        if at + BLOCK < rank:
            h, m, l = split(jnp.concatenate([upper, inverse], axis=1))
            hu, mu, lu = h[:, :rank], m[:, :rank], l[:, :rank]
            lhs = jnp.concatenate([hu, hu, mu, mu, hu, lu], axis=0)
            rhs = jnp.concatenate([h, m, h, m, l, h], axis=0)
            change = lax.dot_general(
                lhs, rhs, (((0,), (0,)), ((), ())), preferred_element_type=F32
            )[at + BLOCK :]
            a = a[BLOCK:] - change[:, :rank]
            e = e[BLOCK:] - change[:, rank:]
    return a, e


def kernel(
    nf, nt, rows_total, cols_total, chunk,
    grad_hbm, mom_hbm, q_ref, mom_out, q_out, scaled_out, right_all,
    grad_ref, mom_ref, buf, q_all, parts, gram, gram_in, gram_all, m_part, m_in, m_all, sq_in,
    qs, qr, ps, pr, gs, gr, hs, hr, ms, mr, fs, fr, ss, sr, local,
):
    f, t = lax.axis_index("fsdp"), lax.axis_index("tp")
    rows, cols = mom_ref.shape
    kr, rank = q_ref.shape[1], q_ref.shape[2]
    gq = rank // nt
    n_chunks = cols // chunk

    def fpeer(d):
        return (lax.rem(f + d, nf), t)

    def tpeer(d):
        return (f, lax.rem(t + d, nt))

    def copy(src, dst, send, recv, d, peer):
        return pltpu.make_async_remote_copy(
            src_ref=src, dst_ref=dst, send_sem=send.at[d], recv_sem=recv.at[d],
            device_id=peer, device_id_type=MESH,
        )

    def q_copy(d):
        return copy(q_ref.at[0], q_all.at[f], qs, qr, d, fpeer(d))

    def p_copy(d):
        return copy(parts.at[t], parts.at[t], ps, pr, d, tpeer(d))

    mine = pl.ds(pl.multiple_of(t * gq, 8), gq)

    def g_copy(d):
        return copy(gram.at[mine], gram_in.at[f], gs, gr, d, fpeer(d))

    def h_copy(d):
        return copy(gram_all.at[t], gram_all.at[t], hs, hr, d, tpeer(d))

    def m_copy(d):
        return copy(m_part.at[lax.rem(f + d, nf)], m_in.at[f], ms, mr, d, fpeer(d))

    def f_copy(d):
        return copy(m_all.at[f], m_all.at[f], fs, fr, d, fpeer(d))

    def s_copy(d):
        return copy(sq_in.at[t], sq_in.at[t], ss, sr, d, tpeer(d))

    def columns(body):
        if n_chunks == 1:
            body(slice(None), slice(None))
        else:
            def step(i, carry):
                at = pl.ds(pl.multiple_of(i * chunk, 128), chunk)
                body(at, at)
                return carry
            lax.fori_loop(0, n_chunks, step, 0)

    grad_copy = pltpu.make_async_copy(grad_hbm, grad_ref, local.at[0])
    mom_copy = pltpu.make_async_copy(mom_hbm, mom_ref, local.at[1])
    own_copy = pltpu.make_async_copy(q_ref.at[0], q_all.at[f], local.at[2])
    own_copy.start()
    mom_copy.start()
    grad_copy.start()

    barrier = pltpu.get_barrier_semaphore()
    each(1, nf, lambda d: pl.semaphore_signal(barrier, inc=1, device_id=fpeer(d), device_id_type=MESH))
    each(1, nt, lambda d: pl.semaphore_signal(barrier, inc=1, device_id=tpeer(d), device_id_type=MESH))
    pl.semaphore_wait(barrier, nf - 1 + nt - 1)

    each(1, nf, lambda d: q_copy(d).start())
    mom_copy.wait()
    grad_copy.wait()
    buf[...] = mom_ref[...] + grad_ref[...].astype(F32)
    own_copy.wait()
    each(1, nf, lambda d: q_copy(d).wait_recv())

    if n_chunks == 1:
        parts[t] = dot(buf[...], q_all[...].reshape(cols, rank), 1, 0)
    else:
        per = chunk // kr
        def left_step(i, total):
            at = pl.ds(pl.multiple_of(i * chunk, 128), chunk)
            return total + dot(buf[:, at], q_all[pl.ds(i * per, per)].reshape(chunk, rank), 1, 0)
        parts[t] = lax.fori_loop(0, n_chunks, left_step, jnp.zeros((rows, rank), F32))
    each(1, nt, lambda d: p_copy(d).start())
    each(1, nt, lambda d: p_copy(d).wait_recv())
    left = sum_slots(parts, nt)

    gram[...] = dot(left, left, 0, 0)
    each(1, nf, lambda d: g_copy(d).start())
    gram_in[f] = gram[mine]

    if n_chunks == 1:
        m_part[...] = dot(buf[...], left, 0, 0).reshape(nf, kr, rank)
    else:
        per = chunk // kr
        def m_step(i, carry):
            at = pl.ds(pl.multiple_of(i * chunk, 128), chunk)
            m_part[pl.ds(i * per, per)] = dot(buf[:, at], left, 0, 0).reshape(per, kr, rank)
            return carry
        lax.fori_loop(0, n_chunks, m_step, 0)
    each(1, nf, lambda d: m_copy(d).start())
    m_in[f] = m_part[f]

    each(1, nf, lambda d: g_copy(d).wait_recv())
    gram_all[t] = sum_slots(gram_in, nf)
    each(1, nt, lambda d: h_copy(d).start())
    each(1, nf, lambda d: m_copy(d).wait_recv())
    m_all[f] = sum_slots(m_in, nf)
    each(1, nf, lambda d: f_copy(d).start())
    each(1, nt, lambda d: h_copy(d).wait_recv())

    a = gram_all[...].reshape(rank, rank)
    row_id = lax.broadcasted_iota(jnp.int32, (rank, rank), 0)
    col_id = lax.broadcasted_iota(jnp.int32, (rank, rank), 1)
    e = jnp.where(row_id == col_id, 1.0, 0.0).astype(F32)
    blocks = rank // BLOCK
    done = []
    a, e = factor_range(a, e, done, 0, blocks // 2)
    factor_range(a, e, done, blocks // 2, blocks)
    inverse = jnp.concatenate(done, axis=0)
    basis = dot(left, inverse, 1, 1)
    each(1, nf, lambda d: f_copy(d).wait_recv())

    if n_chunks == 1:
        right = dot(m_all[...].reshape(cols, rank), inverse, 1, 1)
        right_all[...] = right
        squares = jnp.sum(right * right, axis=0, keepdims=True)
    else:
        per = chunk // kr
        def right_step(i, total):
            at = pl.ds(pl.multiple_of(i * chunk, 128), chunk)
            right = dot(m_all[pl.ds(i * per, per)].reshape(chunk, rank), inverse, 1, 1)
            right_all[at] = right
            return total + jnp.sum(right * right, axis=0, keepdims=True)
        squares = lax.fori_loop(0, n_chunks, right_step, jnp.zeros((1, rank), F32))
    sq_in[t] = jnp.broadcast_to(squares, (8, rank))
    each(1, nt, lambda d: s_copy(d).start())

    def feedback(at, rat):
        mom_out[:, at] = buf[:, at] - 0.05 * dot3(basis, right_all[rat])
    columns(feedback)

    each(1, nt, lambda d: s_copy(d).wait_recv())
    colscale = jnp.sqrt(sum_slots(sq_in, nt)[0:1] / cols_total + 1e-06)
    own = right_all[pl.ds(pl.multiple_of(f * kr, 8), kr)]
    q_out[0] = own / colscale
    scaled_out[...] = basis * ((rows_total / rank) ** 0.5) / colscale

    for c in (q_copy, g_copy, m_copy, f_copy):
        each(1, nf, lambda d: c(d).wait_send())
    for c in (p_copy, h_copy, s_copy):
        each(1, nt, lambda d: c(d).wait_send())


def finish(chunk, mom_ref, q_ref, scaled_ref, right_ref, mom_out, q_out, upd_out, upd, sem):
    mom_copy = pltpu.make_async_copy(mom_ref, mom_out, sem.at[0])
    q_copy = pltpu.make_async_copy(q_ref, q_out, sem.at[1])
    mom_copy.start()
    q_copy.start()
    scaled = scaled_ref[...]
    cols = upd.shape[1]
    if cols == chunk:
        upd[...] = dot3(scaled, right_ref[...]).astype(jnp.bfloat16)
    else:
        def step(i, carry):
            at = pl.ds(pl.multiple_of(i * chunk, 128), chunk)
            upd[:, at] = dot3(scaled, right_ref[at]).astype(jnp.bfloat16)
            return carry
        lax.fori_loop(0, cols // chunk, step, 0)
    upd_copy = pltpu.make_async_copy(upd, upd_out, sem.at[2])
    upd_copy.start()
    mom_copy.wait()
    q_copy.wait()
    upd_copy.wait()


def per_device(nf, nt, gradient, momentum, q_factor):
    rows, cols = momentum.shape
    kr, rank = q_factor.shape[1], q_factor.shape[2]
    chunk = 640 if cols > 640 and cols % 640 == 0 and 640 % kr == 0 else cols
    sem = pltpu.SemaphoreType.DMA
    vmem = pl.BlockSpec(memory_space=pltpu.VMEM)
    hbm = pl.BlockSpec(memory_space=pl.ANY)
    mom, q_new, scaled, right = pl.pallas_call(
        functools.partial(kernel, nf, nt, rows * nf, cols * nt, chunk),
        out_shape=(
            jax.ShapeDtypeStruct((rows, cols), F32),
            jax.ShapeDtypeStruct((1, kr, rank), F32),
            jax.ShapeDtypeStruct((rows, rank), F32),
            jax.ShapeDtypeStruct((cols, rank), F32),
        ),
        in_specs=[pl.BlockSpec(memory_space=pltpu.HBM)] * 3,
        out_specs=(vmem,) * 4,
        scratch_shapes=[
            pltpu.VMEM((rows, cols), jnp.bfloat16),
            pltpu.VMEM((rows, cols), F32),
            pltpu.VMEM((rows, cols), F32),
            pltpu.VMEM((nf, kr, rank), F32),
            pltpu.VMEM((nt, rows, rank), F32),
            pltpu.VMEM((rank, rank), F32),
            pltpu.VMEM((nf, rank // nt, rank), F32),
            pltpu.VMEM((nt, rank // nt, rank), F32),
            pltpu.VMEM((nf, kr, rank), F32),
            pltpu.VMEM((nf, kr, rank), F32),
            pltpu.VMEM((nf, kr, rank), F32),
            pltpu.VMEM((nt, 8, rank), F32),
        ]
        + [sem((nf,)), sem((nf,)), sem((nt,)), sem((nt,)), sem((nf,)), sem((nf,)), sem((nt,)), sem((nt,))]
        + [sem((nf,)), sem((nf,)), sem((nf,)), sem((nf,)), sem((nt,)), sem((nt,)), sem((3,))],
        compiler_params=pltpu.CompilerParams(
            collective_id=0, has_side_effects=True, vmem_limit_bytes=40 * 1024 * 1024
        ),
    )(*[pltpu.with_memory_space_constraint(x, pltpu.HBM) for x in (gradient, momentum, q_factor)])
    return pl.pallas_call(
        functools.partial(finish, chunk),
        out_shape=(
            jax.ShapeDtypeStruct((rows, cols), F32),
            jax.ShapeDtypeStruct((1, kr, rank), F32),
            jax.ShapeDtypeStruct((rows, cols), jnp.bfloat16),
        ),
        in_specs=[vmem] * 4,
        out_specs=(hbm,) * 3,
        scratch_shapes=[pltpu.VMEM((rows, cols), jnp.bfloat16), sem((3,))],
        compiler_params=pltpu.CompilerParams(vmem_limit_bytes=16 * 1024 * 1024),
    )(mom, q_new, scaled, right)


def solution(mesh):
    placed = (P("fsdp", "tp"), P("fsdp", "tp"), P("tp", "fsdp", None))
    return jax.shard_map(
        functools.partial(per_device, mesh.shape["fsdp"], mesh.shape["tp"]),
        mesh=mesh,
        in_specs=placed,
        out_specs=(P("fsdp", "tp"), P("tp", "fsdp", None), P("fsdp", "tp")),
        check_vma=False,
    )
```
